32 devices in a mesh: parts: 2 (over y), expert: 4 (over z), dp: 2 (over x), tensor: 2 (over core).
Axes of the slice: x: 2, y: 2, z: 4, core: 2. Of those that a mesh axis runs over, the one named last changes fastest.
Arguments:
- tokens: bfloat16 [4096, 7168], P(('parts', 'expert', 'tensor'), 'dp'), parts along dimension 0, may hold values from -6 to 6
- cotangent: bfloat16 [4096, 7168], P(('parts', 'expert', 'tensor'), 'dp'), parts along dimension 0, may hold values from -0.59765625 to 0.59765625
- norm_gain: float32 [7168], P('dp'), may hold values from 0.5 to 1.5
- expert_ids: int32 [4096, 1], P(('parts', 'expert', 'tensor')), parts along dimension 0, may hold values from 0 to 1; in each aligned block of 256 rows (0 to 255, 256 to 511, ...) at most 160 rows name the same one
- combine_weight: float32 [4096], P(('parts', 'expert', 'tensor')), parts along dimension 0, may hold values from 0.2 to 1
- up_weight: bfloat16 [7168, 2048], P('dp', ('expert', 'tensor')), may hold values from -0.0625 to 0.0625
- down_weight: bfloat16 [2048, 7168], P(('expert', 'tensor'), 'dp'), may hold values from -0.1875 to 0.1875
Outputs:
- token_grad: bfloat16 [4096, 7168], P(('parts', 'expert', 'tensor'), 'dp'), parts along dimension 0
- up_grad: bfloat16 [14336, 2048], P(('parts', 'dp'), ('expert', 'tensor')), parts along dimension 0
- down_grad: bfloat16 [4096, 7168], P(('parts', 'expert', 'tensor'), 'dp'), parts along dimension 0
- gain_grad: float32 [14336], P(('parts', 'dp')), parts along dimension 0
- token_inner: float32 [4096], P(('parts', 'expert', 'tensor')), parts along dimension 0
The draws below stay inside these ranges and needn't reach their ends.
There are 2 independent parts, one for each index of `parts`. The reference program is written for one: setup_inputs(seed, part) draws one part's arguments, and reference() takes and returns one part's arrays. A program takes and returns all parts, laid end to end along the dimension named above; an argument that names none is the same for every part. Nothing has to cross between parts.
Inputs may be any that keep to these rules, and one draw needn't show every extreme that they name: `expert_ids`: each row names one routed expert. Within the rows of one device (aligned blocks of 256 rows) no expert is named by more than 160 rows, a bound that some block reaches.
All inputs are finite; a program needn't handle non-finite values.
Results may differ from the reference program's by a relative error of at most 0.014.
Values may be sent and summed in bfloat16 or wider, within the bound.
A program may use at most 128 MiB of HBM per device.

```python
import math
import jax
import jax.numpy as jnp
import numpy as np
from jax import lax

D = 7168
FH = 1024
TOP = 1
TOK_DEV = 256
EXPERTS = 2
CAP = 160
TOKENS = 2048
N_DP = 2


def block_scale(rng, shape, pieces, low, top_value):
    factor_of, own = 1.0, jax.random.fold_in(rng, 6)
    for axis_at, parts in pieces:
        steps = jnp.exp(jax.random.uniform(jax.random.fold_in(own, axis_at), (parts,), jnp.float32, low / len(pieces), top_value / len(pieces)))
        factor_of = factor_of * jnp.repeat(steps, shape[axis_at] // parts).reshape([-1 if axis == axis_at else 1 for axis in range(len(shape))])
    return factor_of


def shared_out(own_key, own, number, rows, count, top, bound, lean):
    order = jax.random.permutation(own_key, count)
    packed, ordinary = load_shares(count, rows * top, bound, lean, True), load_shares(count, rows * top, bound, lean, False)
    places = jnp.arange(count)

    def named(lengths, turn):
        used = int((lengths > 0).sum())
        fixed = max(1, used // 4)
        passed = fixed + (places - fixed + turn * (used - fixed)) % max(1, count - fixed)
        return jnp.zeros((count,), jnp.int32).at[order[jnp.where(places < fixed, places, passed)]].set(jnp.asarray(lengths, jnp.int32))

    lengths = jnp.where(number % 4 == 0, named(packed, number // 4), named(ordinary, number - number // 4 - 1))
    mixed = jax.random.permutation(jax.random.fold_in(own, 3), count)
    giver, taker = mixed[0:count // 2 * 2:2], mixed[1:count // 2 * 2:2]
    margin = jnp.minimum(lengths[giver] - 1, bound - lengths[taker]) // 2
    margin = jnp.where((giver == order[0]) | (taker == order[0]) | (lengths[taker] == 0), 0, jnp.maximum(margin, 0))
    passed = jax.random.randint(jax.random.fold_in(own, 4), (count // 2,), 0, 1 << 20) % (margin + 1)
    lengths = lengths.at[giver].add(-passed).at[taker].add(passed)
    items = jnp.searchsorted(jnp.cumsum(lengths), jnp.arange(rows * top), side="right").astype(jnp.int32)
    listing = items.reshape(top, rows).T
    listing = listing[jax.random.permutation(jax.random.fold_in(own, 1), rows)]
    turn = jax.random.randint(jax.random.fold_in(own, 2), (rows, 1), 0, top)
    return jnp.take_along_axis(listing, (jnp.arange(top)[None, :] + turn) % top, axis=1)


def load_shares(number_of, total, reach, skew, full):
    portions = [(1 << 20) // math.isqrt(standing ** skew) + 1 for standing in range(1, number_of + 1)]
    largest = reach if full else min(reach, max(-(-total // number_of), total * portions[0] // sum(portions)))
    least = 1 if total - largest >= number_of - 1 else 0
    holding, surplus = [largest] + [least] * (number_of - 1), total - largest - least * (number_of - 1)
    while surplus > 0:
        free = [i for i in range(1, number_of) if holding[i] < largest] or [i for i in range(1, number_of) if holding[i] < reach]
        mass, left = sum([portions[i] for i in free]), surplus
        for i in free:
            more = min(reach - holding[i], max(1, left * portions[i] // mass), surplus)
            holding[i] = holding[i] + more
            surplus = surplus - more
    return np.array(holding)


def bell_draw(rng, shape, spread, most, split=(), kind=jnp.bfloat16):
    gain = block_scale(rng, shape, split, -0.22, 0.18) if split else 1.0
    entries = jax.random.normal(rng, shape, jnp.float32) * spread * gain
    return jnp.minimum(jnp.maximum(entries, -most), most).astype(kind)


def setup_inputs(seed: int = 0, part: int = 0) -> dict:
    key_of = jax.random.split(jax.random.key(seed), 8)
    part_keys = jax.random.split(jax.random.fold_in(key_of[7], part), 8)
    tokens = bell_draw(part_keys[0], (TOKENS, D), 1.0, 6.0, ((0, 8), (1, 2)))
    cotangent = bell_draw(part_keys[1], (TOKENS, D), 0.1, 0.59765625, ((0, 8), (1, 2)))
    norm_gain = jnp.clip(1.0 + 0.1 * jax.random.normal(key_of[2], (D,), jnp.float32), 0.5, 1.5)
    expert_ids_keys = jax.random.split(jax.random.fold_in(part_keys[3], 1), TOKENS // TOK_DEV)
    expert_ids_turns = jax.random.permutation(jax.random.fold_in(part_keys[3], 3), TOKENS // TOK_DEV)
    expert_ids = jax.vmap(lambda own, number: shared_out(jax.random.fold_in(part_keys[3], 2), own, number, TOK_DEV, EXPERTS, TOP, CAP, 1))(expert_ids_keys, expert_ids_turns).reshape((TOKENS, TOP))
    combine_weight = jnp.clip(0.2 + 0.8 * jax.random.uniform(part_keys[4], (TOKENS,), jnp.float32) ** block_scale(part_keys[4], (TOKENS,), ((0, 8),), -0.2, 0.2), 0.2, 1.0)
    up_weight = bell_draw(key_of[5], (D, EXPERTS * FH), D ** -0.5, 0.0625, ((0, 2), (1, 8)))
    down_weight = bell_draw(key_of[6], (EXPERTS * FH, D), FH ** -0.5, 0.1875, ((0, 8), (1, 2)))
    return {"tokens": tokens, "cotangent": cotangent, "norm_gain": norm_gain, "expert_ids": expert_ids, "combine_weight": combine_weight, "up_weight": up_weight, "down_weight": down_weight}


def slope(pre):
    sig = jax.nn.sigmoid(pre)
    return sig * (1.0 + pre * (1.0 - sig))

def sliced_sum(rows, weight_block, form):
    blocks = rows.reshape(rows.shape[0], N_DP, D // N_DP).astype(jnp.float32)
    products = jnp.einsum(form, blocks, weight_block.astype(jnp.float32))
    rounded = lax.optimization_barrier(products.astype(jnp.bfloat16))
    return lax.optimization_barrier(jnp.sum(rounded.astype(jnp.float32), axis=1))

def contract(left, right, left_dim, right_dim):
    return lax.dot_general(left, right, (((left_dim,), (right_dim,)), ((), ())), preferred_element_type=jnp.float32)

def reference(tokens, cotangent, norm_gain, expert_ids, combine_weight, up_weight, down_weight):
    groups = TOKENS // TOK_DEV
    half = FH // 2
    token_f = tokens.astype(jnp.float32)
    scale = lax.rsqrt(lax.optimization_barrier(jnp.mean(token_f * token_f, axis=1, keepdims=True)) + 1e-06)
    normed = (token_f * scale * norm_gain[None, :]).astype(jnp.bfloat16)
    scaled = (combine_weight[:, None] * cotangent.astype(jnp.float32)).astype(jnp.bfloat16)
    target = expert_ids[:, 0].reshape(groups, TOK_DEV)
    hits = (target[:, :, None] == jnp.arange(EXPERTS, dtype=jnp.int32)[None, None, :]).astype(jnp.int32)
    slot = lax.optimization_barrier(jnp.sum((jnp.cumsum(hits, axis=1) - 1) * hits, axis=2)).astype(jnp.int32)
    index = jnp.arange(TOKENS, dtype=jnp.int32).reshape(groups, TOK_DEV)
    owner = jnp.broadcast_to(jnp.arange(groups, dtype=jnp.int32)[:, None], (groups, TOK_DEV))
    table = jnp.zeros((groups, EXPERTS, CAP), jnp.int32).at[owner, target, slot].set(index + 1)

    def expert_terms(expert):
        picks = lax.dynamic_index_in_dim(table, expert, 1, keepdims=False).reshape(-1)
        valid = (picks > 0)[:, None]
        rows = jnp.maximum(picks - 1, 0).astype(jnp.int32)
        rows_x = jnp.where(valid, normed[rows], jnp.zeros((), jnp.bfloat16))
        rows_d = jnp.where(valid, scaled[rows], jnp.zeros((), jnp.bfloat16))
        start = (expert * FH).astype(jnp.int32)
        w_up = lax.dynamic_slice_in_dim(up_weight, start, FH, 1)
        w_down = lax.dynamic_slice_in_dim(down_weight, start, FH, 0)
        pre = sliced_sum(rows_x, w_up.reshape(N_DP, D // N_DP, FH), 'rsk,skh->rsh')
        back = sliced_sum(rows_d, w_down.reshape(FH, N_DP, D // N_DP), 'rsk,hsk->rsh')
        act = jax.nn.silu(pre).astype(jnp.bfloat16)
        dpre = (back * slope(pre)).astype(jnp.bfloat16)
        down_g = contract(act, rows_d, 0, 0).astype(jnp.bfloat16)
        up_g = contract(rows_x, dpre, 0, 0).astype(jnp.bfloat16)
        lower = lax.optimization_barrier(contract(dpre[:, :half], w_up[:, :half], 1, 1).astype(jnp.bfloat16))
        upper = lax.optimization_barrier(contract(dpre[:, half:], w_up[:, half:], 1, 1).astype(jnp.bfloat16))
        return (up_g, down_g, lower.astype(jnp.float32) + upper.astype(jnp.float32), rows)
    up_all, down_all, terms, rows_all = lax.map(expert_terms, jnp.arange(EXPERTS, dtype=jnp.int32))
    normed_grad = jnp.zeros((TOKENS, D), jnp.float32).at[rows_all.reshape(-1)].add(terms.reshape(-1, D))
    up_grad = up_all.transpose(1, 0, 2).reshape(D, EXPERTS * FH)
    down_grad = down_all.reshape(EXPERTS * FH, D)
    gain_grad = lax.optimization_barrier(jnp.sum(normed_grad * token_f * scale, axis=0))
    inner = lax.optimization_barrier(jnp.sum(token_f * norm_gain[None, :] * normed_grad, axis=1, keepdims=True))
    cubed = scale * scale * scale
    token_grad = cotangent.astype(jnp.float32) + scale * norm_gain[None, :] * normed_grad - token_f * cubed * inner / D
    return (token_grad.astype(jnp.bfloat16), up_grad, down_grad, gain_grad, inner[:, 0])
```

```python
import jax
import jax.numpy as jnp
from jax import lax
from jax.sharding import PartitionSpec as P


def slope(pre):
    sig = jax.nn.sigmoid(pre)
    return sig * (1.0 + pre * (1.0 - sig))


def contract(left, right, left_dim, right_dim):
    return lax.dot_general(
        left, right, (((left_dim,), (right_dim,)), ((), ())), preferred_element_type=jnp.float32
    )


def local(tokens, cotangent, norm_gain, expert_ids, combine_weight, up_weight, down_weight):
    n_expert = lax.axis_size("expert")
    groups = n_expert // 2
    count, piece = tokens.shape
    width = piece * lax.axis_size("dp")
    capacity = count * 5 // (4 * groups)
    token_f = tokens.astype(jnp.float32)
    squares = lax.psum(jnp.sum(token_f * token_f, axis=1, keepdims=True), "dp")
    scale = lax.rsqrt(squares / width + 1e-06)
    normed = (token_f * scale * norm_gain[None, :]).astype(jnp.bfloat16)
    scaled = (combine_weight[:, None] * cotangent.astype(jnp.float32)).astype(jnp.bfloat16)
    target = expert_ids[:, 0]
    hits = (target[:, None] == jnp.arange(groups, dtype=jnp.int32)[None, :]).astype(jnp.int32)
    slot = jnp.sum((jnp.cumsum(hits, axis=0) - 1) * hits, axis=1)
    flat_slot = target * capacity + slot
    places = (flat_slot[:, None] == jnp.arange(groups * capacity, dtype=jnp.int32)[None, :]).astype(
        jnp.bfloat16
    )
    packed_x = contract(places, normed, 0, 0).astype(jnp.bfloat16)
    packed_d = contract(places, scaled, 0, 0).astype(jnp.bfloat16)

    def outward(packed):
        return jnp.repeat(packed.reshape(groups, capacity, piece), 2, axis=0)

    sent_x, sent_d = (
        lax.all_to_all(outward(packed_x), "expert", split_axis=0, concat_axis=0, tiled=True),
        lax.all_to_all(outward(packed_d), "expert", split_axis=0, concat_axis=0, tiled=True),
    )
    rows_x = sent_x.reshape(-1, piece)
    rows_d = sent_d.reshape(-1, piece)
    full_up, full_down = (
        lax.all_gather(up_weight, "tensor", axis=1, tiled=True),
        lax.all_gather(down_weight, "tensor", axis=0, tiled=True),
    )
    up_part = jnp.dot(rows_x, full_up, preferred_element_type=jnp.float32)
    back_part = contract(rows_d, full_down, 1, 1)
    pre, back = (
        lax.psum(up_part.astype(jnp.bfloat16), "dp").astype(jnp.float32),
        lax.psum(back_part.astype(jnp.bfloat16), "dp").astype(jnp.float32),
    )
    act = jax.nn.silu(pre).astype(jnp.bfloat16)
    dpre = (back * slope(pre)).astype(jnp.bfloat16)
    down_terms = contract(act, rows_d, 0, 0)
    up_terms = contract(rows_x, dpre, 0, 0)
    down_sum, up_sum = (
        lax.psum_scatter(
            down_terms.astype(jnp.bfloat16), "tensor", scatter_dimension=0, tiled=True
        ).astype(jnp.float32),
        lax.psum_scatter(
            up_terms.astype(jnp.bfloat16), "tensor", scatter_dimension=1, tiled=True
        ).astype(jnp.float32),
    )
    down_grad = down_sum.astype(jnp.bfloat16)
    up_grad = up_sum.astype(jnp.bfloat16)
    row_grad = contract(dpre, full_up, 1, 1).astype(jnp.bfloat16)
    returned = lax.all_to_all(
        row_grad.reshape(n_expert, capacity, piece),
        "expert",
        split_axis=0,
        concat_axis=0,
        tiled=True,
    )
    returned = returned.reshape(groups, 2, capacity, piece).astype(jnp.float32)
    merged = (returned[:, 0] + returned[:, 1]).reshape(groups * capacity, piece)
    normed_grad = jnp.take(merged, flat_slot, axis=0)
    gain_terms = jnp.sum(normed_grad * token_f * scale, axis=0)
    gain_grad = lax.psum(gain_terms, ("expert", "tensor"))
    inner_part = jnp.sum(token_f * norm_gain[None, :] * normed_grad, axis=1, keepdims=True)
    inner = lax.psum(inner_part, "dp")
    cubed = scale * scale * scale
    token_grad = (
        cotangent.astype(jnp.float32)
        + scale * norm_gain[None, :] * normed_grad
        - token_f * cubed * inner / width
    )
    return (token_grad.astype(jnp.bfloat16), up_grad, down_grad, gain_grad, inner[:, 0])


def after(value, *earlier):
    return lax.optimization_barrier((value,) + earlier)[0]


def swap(value, axis):
    return lax.ppermute(value, axis, ((0, 1), (1, 0)))


def local_line(
    tokens, cotangent, norm_gain, expert_ids, combine_weight, up_weight, down_weight
):
    count, piece = tokens.shape
    width = piece * 2
    capacity = count * 5 // 8
    inward, middle, outward = ((0, 1), (3, 2)), ((1, 2), (2, 1)), ((1, 0), (2, 3))
    place = lax.axis_index("expert")
    mine = place // 2
    is_inner = (place == 1) | (place == 2)
    part = lax.axis_index("parts")

    tokens_in = lax.ppermute(tokens, "expert", inward)
    half_up = lax.dynamic_slice_in_dim(up_weight, part * (piece // 2), piece // 2, 0)
    rows_down = down_weight.shape[0] // 2
    half_down = lax.dynamic_slice_in_dim(down_weight, part * rows_down, rows_down, 0)
    half_up = lax.ppermute(after(half_up, tokens_in), "expert", inward)
    cotangent_in = lax.ppermute(after(cotangent, half_up), "expert", inward)
    half_down = lax.ppermute(after(half_down, cotangent_in), "expert", inward)

    token_f = tokens.astype(jnp.float32)
    squares = lax.psum(jnp.sum(token_f * token_f, axis=1), "dp")
    scale = lax.rsqrt(squares / width + 1e-06)
    target = expert_ids[:, 0]
    small = jnp.stack([scale, combine_weight, target.astype(jnp.float32)])
    small_in = lax.ppermute(small, "expert", inward)

    def pack(block, cot_block, facts):
        scale_b, gate_b = facts[0][:, None], facts[1][:, None]
        target_b = facts[2].astype(jnp.int32)
        normed = (block.astype(jnp.float32) * scale_b * norm_gain[None, :]).astype(jnp.bfloat16)
        scaled = (gate_b * cot_block.astype(jnp.float32)).astype(jnp.bfloat16)

        def places(expert):
            hit = target_b == expert
            slot = jnp.where(hit, jnp.cumsum(hit.astype(jnp.int32)) - 1, -1)
            return (slot[:, None] == jnp.arange(capacity, dtype=jnp.int32)[None, :]).astype(
                jnp.bfloat16
            )

        keep, send = places(mine), places(1 - mine)

        def picked(where, rows):
            return contract(where, rows, 0, 0).astype(jnp.bfloat16)

        return keep, send, normed, scaled, picked

    keep_a, send_a, normed_a, scaled_a, picked = pack(tokens, cotangent, small)
    keep_b, send_b, normed_b, scaled_b, picked = pack(tokens_in, cotangent_in, small_in)
    far_xa = lax.ppermute(picked(send_a, normed_a), "expert", middle)
    far_da = lax.ppermute(picked(send_a, scaled_a), "expert", middle)
    far_xb = lax.ppermute(picked(send_b, normed_b), "expert", middle)
    far_db = lax.ppermute(picked(send_b, scaled_b), "expert", middle)

    def joined(half, own, axis):
        other = swap(half, "parts")
        first = jnp.where(part == 0, half, other)
        second = jnp.where(part == 0, other, half)
        outer = jnp.concatenate([first, second], axis=0)
        both = jnp.concatenate([own, outer], axis=axis)
        return lax.all_gather(both, "tensor", axis=axis, tiled=True)

    full_up = joined(half_up, up_weight, 1)
    full_down = joined(half_down, down_weight, 0)
    rows_x = jnp.concatenate([far_xa, far_xb, picked(keep_a, normed_a), picked(keep_b, normed_b)])
    rows_d = jnp.concatenate([far_da, far_db, picked(keep_a, scaled_a), picked(keep_b, scaled_b)])

    def over_dp(value):
        rounded = value.astype(jnp.bfloat16)
        return rounded.astype(jnp.float32) + swap(rounded, "dp").astype(jnp.float32)

    pre = over_dp(contract(rows_x, full_up, 1, 0))
    back = over_dp(contract(rows_d, full_down, 1, 1))
    act = jax.nn.silu(pre).astype(jnp.bfloat16)
    dpre = (back * slope(pre)).astype(jnp.bfloat16)
    span = 2 * capacity
    far_grad = contract(dpre[:span], full_up, 1, 1).astype(jnp.bfloat16)
    back_b = lax.ppermute(far_grad[capacity:], "expert", middle)
    back_a = lax.ppermute(far_grad[:capacity], "expert", middle)
    near_grad = contract(dpre[span:], full_up, 1, 1).astype(jnp.bfloat16)

    def restored(keep, near, send, far):
        return (contract(keep, near, 1, 0) + contract(send, far, 1, 0)).astype(jnp.bfloat16)

    grad_b = restored(keep_b, near_grad[capacity:], send_b, back_b)
    grad_in = lax.ppermute(grad_b, "expert", outward)
    grad_a = restored(keep_a, near_grad[:capacity], send_a, back_a)

    side = lax.axis_index("tensor")

    def shared(terms, axis):
        size = terms.shape[axis] // 2
        own = lax.dynamic_slice_in_dim(terms, side * size, size, axis)
        other = lax.dynamic_slice_in_dim(terms, (1 - side) * size, size, axis)
        total = own + swap(other.astype(jnp.bfloat16), "tensor").astype(jnp.float32)
        total = total.astype(jnp.bfloat16)
        inner_half, outer_half = jnp.split(total, 2, axis=axis)
        arrived = lax.ppermute(outer_half, "expert", outward)
        return jnp.where(is_inner, inner_half, arrived)

    down_grad = shared(contract(act, rows_d, 0, 0), 0)
    up_grad = shared(contract(rows_x, dpre, 0, 0), 1)

    normed_grad = jnp.where(is_inner, grad_a, grad_in).astype(jnp.float32)
    scale = scale[:, None]
    gain_grad = lax.psum(jnp.sum(normed_grad * token_f * scale, axis=0), ("expert", "tensor"))
    inner_part = jnp.sum(token_f * norm_gain[None, :] * normed_grad, axis=1)
    inner = lax.psum(inner_part, "dp")
    cubed = scale * scale * scale
    token_grad = (
        cotangent.astype(jnp.float32)
        + scale * norm_gain[None, :] * normed_grad
        - token_f * cubed * inner[:, None] / width
    )
    return (token_grad.astype(jnp.bfloat16), up_grad, down_grad, gain_grad, inner)


def solution(mesh):
    sizes = tuple(mesh.shape[name] for name in ("parts", "expert", "dp", "tensor"))
    body = local_line if sizes == (2, 4, 2, 2) else local
    in_specs = (
        P(("parts", "expert", "tensor"), "dp"),
        P(("parts", "expert", "tensor"), "dp"),
        P("dp"),
        P(("parts", "expert", "tensor"), None),
        P(("parts", "expert", "tensor")),
        P("dp", ("expert", "tensor")),
        P(("expert", "tensor"), "dp"),
    )
    out_specs = (
        P(("parts", "expert", "tensor"), "dp"),
        P(("parts", "dp"), ("expert", "tensor")),
        P(("parts", "expert", "tensor"), "dp"),
        P(("parts", "dp")),
        P(("parts", "expert", "tensor")),
    )
    return jax.shard_map(body, mesh=mesh, in_specs=in_specs, out_specs=out_specs, check_vma=False)
```

```python
import jax
import jax.numpy as jnp
from jax import lax
from jax.sharding import PartitionSpec as P


def slope(pre):
    sig = jax.nn.sigmoid(pre)
    return sig * (1.0 + pre * (1.0 - sig))


def contract(left, right, left_dim, right_dim):
    return lax.dot_general(
        left, right, (((left_dim,), (right_dim,)), ((), ())), preferred_element_type=jnp.float32
    )


def local(tokens, cotangent, norm_gain, expert_ids, combine_weight, up_weight, down_weight):
    n_expert = lax.axis_size("expert")
    groups = n_expert // 2
    count, piece = tokens.shape
    width = piece * lax.axis_size("dp")
    capacity = count * 5 // (4 * groups)
    token_f = tokens.astype(jnp.float32)
    squares = lax.psum(jnp.sum(token_f * token_f, axis=1, keepdims=True), "dp")
    scale = lax.rsqrt(squares / width + 1e-06)
    normed = (token_f * scale * norm_gain[None, :]).astype(jnp.bfloat16)
    scaled = (combine_weight[:, None] * cotangent.astype(jnp.float32)).astype(jnp.bfloat16)
    target = expert_ids[:, 0]
    hits = (target[:, None] == jnp.arange(groups, dtype=jnp.int32)[None, :]).astype(jnp.int32)
    slot = jnp.sum((jnp.cumsum(hits, axis=0) - 1) * hits, axis=1)
    flat_slot = target * capacity + slot
    places = (flat_slot[:, None] == jnp.arange(groups * capacity, dtype=jnp.int32)[None, :]).astype(
        jnp.bfloat16
    )
    packed_x = contract(places, normed, 0, 0).astype(jnp.bfloat16)
    packed_d = contract(places, scaled, 0, 0).astype(jnp.bfloat16)

    def outward(packed):
        return jnp.repeat(packed.reshape(groups, capacity, piece), 2, axis=0)

    sent_x, sent_d = (
        lax.all_to_all(outward(packed_x), "expert", split_axis=0, concat_axis=0, tiled=True),
        lax.all_to_all(outward(packed_d), "expert", split_axis=0, concat_axis=0, tiled=True),
    )
    rows_x = sent_x.reshape(-1, piece)
    rows_d = sent_d.reshape(-1, piece)
    full_up, full_down = (
        lax.all_gather(up_weight, "tensor", axis=1, tiled=True),
        lax.all_gather(down_weight, "tensor", axis=0, tiled=True),
    )
    up_part = jnp.dot(rows_x, full_up, preferred_element_type=jnp.float32)
    back_part = contract(rows_d, full_down, 1, 1)
    pre, back = (
        lax.psum(up_part.astype(jnp.bfloat16), "dp").astype(jnp.float32),
        lax.psum(back_part.astype(jnp.bfloat16), "dp").astype(jnp.float32),
    )
    act = jax.nn.silu(pre).astype(jnp.bfloat16)
    dpre = (back * slope(pre)).astype(jnp.bfloat16)
    down_terms = contract(act, rows_d, 0, 0)
    up_terms = contract(rows_x, dpre, 0, 0)
    down_sum, up_sum = (
        lax.psum_scatter(
            down_terms.astype(jnp.bfloat16), "tensor", scatter_dimension=0, tiled=True
        ).astype(jnp.float32),
        lax.psum_scatter(
            up_terms.astype(jnp.bfloat16), "tensor", scatter_dimension=1, tiled=True
        ).astype(jnp.float32),
    )
    down_grad = down_sum.astype(jnp.bfloat16)
    up_grad = up_sum.astype(jnp.bfloat16)
    row_grad = contract(dpre, full_up, 1, 1).astype(jnp.bfloat16)
    returned = lax.all_to_all(
        row_grad.reshape(n_expert, capacity, piece),
        "expert",
        split_axis=0,
        concat_axis=0,
        tiled=True,
    )
    returned = returned.reshape(groups, 2, capacity, piece).astype(jnp.float32)
    merged = (returned[:, 0] + returned[:, 1]).reshape(groups * capacity, piece)
    normed_grad = jnp.take(merged, flat_slot, axis=0)
    gain_terms = jnp.sum(normed_grad * token_f * scale, axis=0)
    gain_grad = lax.psum(gain_terms, ("expert", "tensor"))
    inner_part = jnp.sum(token_f * norm_gain[None, :] * normed_grad, axis=1, keepdims=True)
    inner = lax.psum(inner_part, "dp")
    cubed = scale * scale * scale
    token_grad = (
        cotangent.astype(jnp.float32)
        + scale * norm_gain[None, :] * normed_grad
        - token_f * cubed * inner / width
    )
    return (token_grad.astype(jnp.bfloat16), up_grad, down_grad, gain_grad, inner[:, 0])


def swap(value, axis):
    return lax.ppermute(value, axis, ((0, 1), (1, 0)))


def tie(*values):
    return lax.optimization_barrier(values)


def rounded(value):
    return value.astype(jnp.bfloat16)


def local_line(
    tokens, cotangent, norm_gain, expert_ids, combine_weight, up_weight, down_weight
):
    count, piece = tokens.shape
    width = piece * 2
    capacity = count * 5 // 8
    inward, middle, outward = ((0, 1), (3, 2)), ((1, 2), (2, 1)), ((1, 0), (2, 3))
    place = lax.axis_index("expert")
    mine = place // 2
    is_inner = (place == 1) | (place == 2)
    part = lax.axis_index("parts")
    side = lax.axis_index("tensor")

    def along(value, pairs):
        return lax.ppermute(value, "expert", pairs)

    def half(weight):
        size = weight.shape[0] // 2
        return lax.dynamic_slice_in_dim(weight, part * size, size, 0)

    tokens_in = along(tokens, inward)
    up_own = lax.all_gather(up_weight, "tensor", axis=1, tiled=True)
    down_own = lax.all_gather(down_weight, "tensor", axis=0, tiled=True)
    token_f = tokens.astype(jnp.float32)
    squares = lax.psum(jnp.sum(token_f * token_f, axis=1), "dp")
    scale = lax.rsqrt(squares / width + 1e-06)
    small = jnp.stack([scale, combine_weight, expert_ids[:, 0].astype(jnp.float32)])
    small_in = along(small, inward)

    def places(facts, expert):
        hit = facts[2].astype(jnp.int32) == expert
        slot = jnp.where(hit, jnp.cumsum(hit.astype(jnp.int32)) - 1, -1)
        return rounded(slot[:, None] == jnp.arange(capacity, dtype=jnp.int32)[None, :])

    def normed_of(block, facts):
        return rounded(block.astype(jnp.float32) * facts[0][:, None] * norm_gain[None, :])

    def scaled_of(block, facts):
        return rounded(facts[1][:, None] * block.astype(jnp.float32))

    def picked(where, rows):
        return rounded(contract(where, rows, 0, 0))

    keep_a, send_a = places(small, mine), places(small, 1 - mine)
    normed_a, scaled_a = normed_of(tokens, small), scaled_of(cotangent, small)
    far_xa = along(picked(send_a, normed_a), middle)
    near_xa, near_da = picked(keep_a, normed_a), picked(keep_a, scaled_a)
    send_da = picked(send_a, scaled_a)
    half_up, tokens_in, far_xa, send_da, near_xa, near_da, small_in = tie(
        half(up_weight), tokens_in, far_xa, send_da, near_xa, near_da, small_in
    )

    up_in = along(half_up, inward)
    far_da = along(send_da, middle)
    keep_b, send_b = places(small_in, mine), places(small_in, 1 - mine)
    normed_b = normed_of(tokens_in, small_in)
    send_xb, near_xb = picked(send_b, normed_b), picked(keep_b, normed_b)
    half_down, up_in, far_da, send_xb, near_xb = tie(
        half(down_weight), up_in, far_da, send_xb, near_xb
    )

    down_in = along(half_down, inward)
    far_xb = along(send_xb, middle)
    up_out = lax.all_gather(up_in, "parts", axis=0, tiled=True)
    cot_sent, down_in, far_xb, up_out = tie(cotangent, down_in, far_xb, up_out)

    cotangent_in = along(cot_sent, inward)
    up_out = lax.all_gather(up_out, "tensor", axis=1, tiled=True)
    down_out = lax.all_gather(down_in, "parts", axis=0, tiled=True)
    down_out = lax.all_gather(down_out, "tensor", axis=0, tiled=True)
    rows_x = jnp.concatenate([far_xa, near_xa, near_xb, far_xb])

    def over_dp(value):
        return value.astype(jnp.float32) + swap(value, "dp").astype(jnp.float32)

    pre_own = rounded(contract(rows_x, up_own, 1, 0))
    pre_out = rounded(contract(rows_x, up_out, 1, 0))
    pre = jnp.concatenate([over_dp(pre_own), over_dp(pre_out)], axis=1)
    cotangent_in, pre_out, down_out = tie(cotangent_in, pre_out, down_out)

    scaled_b = scaled_of(cotangent_in, small_in)
    far_db = along(picked(send_b, scaled_b), middle)
    early = jnp.concatenate([far_da, near_da, picked(keep_b, scaled_b)])

    def back_of(rows):
        parts_of = [contract(rows, down_own, 1, 1), contract(rows, down_out, 1, 1)]
        return over_dp(rounded(jnp.concatenate(parts_of, axis=1)))

    back = jnp.concatenate([back_of(early), back_of(far_db)])
    rows_d = jnp.concatenate([early, far_db])
    act = rounded(jax.nn.silu(pre))
    dpre = rounded(back * slope(pre))
    unit = act.shape[1] // 2

    def row_grad(rows):
        own = contract(rows[:, :unit], up_own, 1, 1)
        return rounded(own + contract(rows[:, unit:], up_out, 1, 1))

    back_b = along(row_grad(dpre[3 * capacity :]), middle)
    back_a = along(row_grad(dpre[:capacity]), middle)
    near_grad = row_grad(dpre[capacity : 3 * capacity])

    def shared(terms, axis):
        size = terms.shape[axis] // 2
        own = lax.dynamic_slice_in_dim(terms, side * size, size, axis)
        other = lax.dynamic_slice_in_dim(terms, (1 - side) * size, size, axis)
        return rounded(own + swap(rounded(other), "tensor").astype(jnp.float32))

    down_far = along(shared(contract(act[:, unit:], rows_d, 0, 0), 0), outward)
    up_far = along(shared(contract(rows_x, dpre[:, unit:], 0, 0), 1), outward)
    down_near = shared(contract(act[:, :unit], rows_d, 0, 0), 0)
    up_near = shared(contract(rows_x, dpre[:, :unit], 0, 0), 1)

    def restored(keep, near, send, far):
        return rounded(contract(keep, near, 1, 0) + contract(send, far, 1, 0))

    grad_b = restored(keep_b, near_grad[capacity:], send_b, back_b)
    grad_in = along(grad_b, outward)
    grad_a = restored(keep_a, near_grad[:capacity], send_a, back_a)

    def gain_of(grad, block, facts):
        block = block.astype(jnp.float32) * facts[0][:, None]
        return jnp.sum(grad.astype(jnp.float32) * block, axis=0)

    def inner_of(grad, block):
        gained = block.astype(jnp.float32) * norm_gain[None, :]
        return jnp.sum(gained * grad.astype(jnp.float32), axis=1)

    gain_terms = gain_of(grad_a, tokens, small) + gain_of(grad_b, tokens_in, small_in)
    gain_grad = lax.psum(jnp.where(is_inner, gain_terms, 0.0), ("expert", "tensor"))
    inner_ab = jnp.stack([inner_of(grad_a, tokens), inner_of(grad_b, tokens_in)])
    inner_ab = over_dp(inner_ab)
    inner = jnp.where(is_inner, inner_ab[0], along(inner_ab[1], outward))
    normed_grad = jnp.where(is_inner, grad_a, grad_in).astype(jnp.float32)
    scale = scale[:, None]
    cubed = scale * scale * scale
    token_grad = (
        cotangent.astype(jnp.float32)
        + scale * norm_gain[None, :] * normed_grad
        - token_f * cubed * inner[:, None] / width
    )
    up_grad = jnp.where(is_inner, up_near, up_far)
    down_grad = jnp.where(is_inner, down_near, down_far)
    return (rounded(token_grad), up_grad, down_grad, gain_grad, inner)


def solution(mesh):
    sizes = tuple(mesh.shape[name] for name in ("parts", "expert", "dp", "tensor"))
    body = local_line if sizes == (2, 4, 2, 2) else local
    in_specs = (
        P(("parts", "expert", "tensor"), "dp"),
        P(("parts", "expert", "tensor"), "dp"),
        P("dp"),
        P(("parts", "expert", "tensor"), None),
        P(("parts", "expert", "tensor")),
        P("dp", ("expert", "tensor")),
        P(("expert", "tensor"), "dp"),
    )
    out_specs = (
        P(("parts", "expert", "tensor"), "dp"),
        P(("parts", "dp"), ("expert", "tensor")),
        P(("parts", "expert", "tensor"), "dp"),
        P(("parts", "dp")),
        P(("parts", "expert", "tensor")),
    )
    return jax.shard_map(body, mesh=mesh, in_specs=in_specs, out_specs=out_specs, check_vma=False)
```

```python
import jax
import jax.numpy as jnp
from jax import lax
from jax.sharding import PartitionSpec as P


def slope(pre):
    sig = jax.nn.sigmoid(pre)
    return sig * (1.0 + pre * (1.0 - sig))


def contract(left, right, left_dim, right_dim):
    return lax.dot_general(
        left, right, (((left_dim,), (right_dim,)), ((), ())), preferred_element_type=jnp.float32
    )


def local(tokens, cotangent, norm_gain, expert_ids, combine_weight, up_weight, down_weight):
    n_expert = lax.axis_size("expert")
    groups = n_expert // 2
    count, piece = tokens.shape
    width = piece * lax.axis_size("dp")
    capacity = count * 5 // (4 * groups)
    token_f = tokens.astype(jnp.float32)
    squares = lax.psum(jnp.sum(token_f * token_f, axis=1, keepdims=True), "dp")
    scale = lax.rsqrt(squares / width + 1e-06)
    normed = (token_f * scale * norm_gain[None, :]).astype(jnp.bfloat16)
    scaled = (combine_weight[:, None] * cotangent.astype(jnp.float32)).astype(jnp.bfloat16)
    target = expert_ids[:, 0]
    hits = (target[:, None] == jnp.arange(groups, dtype=jnp.int32)[None, :]).astype(jnp.int32)
    slot = jnp.sum((jnp.cumsum(hits, axis=0) - 1) * hits, axis=1)
    flat_slot = target * capacity + slot
    places = (flat_slot[:, None] == jnp.arange(groups * capacity, dtype=jnp.int32)[None, :]).astype(
        jnp.bfloat16
    )
    packed_x = contract(places, normed, 0, 0).astype(jnp.bfloat16)
    packed_d = contract(places, scaled, 0, 0).astype(jnp.bfloat16)

    def outward(packed):
        return jnp.repeat(packed.reshape(groups, capacity, piece), 2, axis=0)

    sent_x, sent_d = (
        lax.all_to_all(outward(packed_x), "expert", split_axis=0, concat_axis=0, tiled=True),
        lax.all_to_all(outward(packed_d), "expert", split_axis=0, concat_axis=0, tiled=True),
    )
    rows_x = sent_x.reshape(-1, piece)
    rows_d = sent_d.reshape(-1, piece)
    full_up, full_down = (
        lax.all_gather(up_weight, "tensor", axis=1, tiled=True),
        lax.all_gather(down_weight, "tensor", axis=0, tiled=True),
    )
    up_part = jnp.dot(rows_x, full_up, preferred_element_type=jnp.float32)
    back_part = contract(rows_d, full_down, 1, 1)
    pre, back = (
        lax.psum(up_part.astype(jnp.bfloat16), "dp").astype(jnp.float32),
        lax.psum(back_part.astype(jnp.bfloat16), "dp").astype(jnp.float32),
    )
    act = jax.nn.silu(pre).astype(jnp.bfloat16)
    dpre = (back * slope(pre)).astype(jnp.bfloat16)
    down_terms = contract(act, rows_d, 0, 0)
    up_terms = contract(rows_x, dpre, 0, 0)
    down_sum, up_sum = (
        lax.psum_scatter(
            down_terms.astype(jnp.bfloat16), "tensor", scatter_dimension=0, tiled=True
        ).astype(jnp.float32),
        lax.psum_scatter(
            up_terms.astype(jnp.bfloat16), "tensor", scatter_dimension=1, tiled=True
        ).astype(jnp.float32),
    )
    down_grad = down_sum.astype(jnp.bfloat16)
    up_grad = up_sum.astype(jnp.bfloat16)
    row_grad = contract(dpre, full_up, 1, 1).astype(jnp.bfloat16)
    returned = lax.all_to_all(
        row_grad.reshape(n_expert, capacity, piece),
        "expert",
        split_axis=0,
        concat_axis=0,
        tiled=True,
    )
    returned = returned.reshape(groups, 2, capacity, piece).astype(jnp.float32)
    merged = (returned[:, 0] + returned[:, 1]).reshape(groups * capacity, piece)
    normed_grad = jnp.take(merged, flat_slot, axis=0)
    gain_terms = jnp.sum(normed_grad * token_f * scale, axis=0)
    gain_grad = lax.psum(gain_terms, ("expert", "tensor"))
    inner_part = jnp.sum(token_f * norm_gain[None, :] * normed_grad, axis=1, keepdims=True)
    inner = lax.psum(inner_part, "dp")
    cubed = scale * scale * scale
    token_grad = (
        cotangent.astype(jnp.float32)
        + scale * norm_gain[None, :] * normed_grad
        - token_f * cubed * inner / width
    )
    return (token_grad.astype(jnp.bfloat16), up_grad, down_grad, gain_grad, inner[:, 0])


def swap(value, axis):
    return lax.ppermute(value, axis, ((0, 1), (1, 0)))


def tie(*values):
    return lax.optimization_barrier(values)


def rounded(value):
    return value.astype(jnp.bfloat16)


def local_line(
    tokens, cotangent, norm_gain, expert_ids, combine_weight, up_weight, down_weight
):
    count, piece = tokens.shape
    width = piece * 2
    capacity = count * 5 // 8
    inward, middle, outward = ((0, 1), (3, 2)), ((1, 2), (2, 1)), ((1, 0), (2, 3))
    place = lax.axis_index("expert")
    mine = place // 2
    is_inner = (place == 1) | (place == 2)
    part = lax.axis_index("parts")
    side = lax.axis_index("tensor")

    def along(value, pairs):
        return lax.ppermute(value, "expert", pairs)

    def half(weight):
        size = weight.shape[0] // 2
        return lax.dynamic_slice_in_dim(weight, part * size, size, 0)

    tokens_in = along(tokens, inward)
    up_own = lax.all_gather(up_weight, "tensor", axis=1, tiled=True)
    down_own = lax.all_gather(down_weight, "tensor", axis=0, tiled=True)
    token_f = tokens.astype(jnp.float32)
    squares = lax.psum(jnp.sum(token_f * token_f, axis=1), "dp")
    scale = lax.rsqrt(squares / width + 1e-06)
    small = jnp.stack([scale, combine_weight, expert_ids[:, 0].astype(jnp.float32)])
    small_in = along(small, inward)

    def places(facts, expert):
        hit = facts[2].astype(jnp.int32) == expert
        slot = jnp.where(hit, jnp.cumsum(hit.astype(jnp.int32)) - 1, -1)
        return rounded(slot[:, None] == jnp.arange(capacity, dtype=jnp.int32)[None, :])

    def normed_of(block, facts):
        return rounded(block.astype(jnp.float32) * facts[0][:, None] * norm_gain[None, :])

    def scaled_of(block, facts):
        return rounded(facts[1][:, None] * block.astype(jnp.float32))

    def picked(where, rows):
        return rounded(contract(where, rows, 0, 0))

    keep_a, send_a = places(small, mine), places(small, 1 - mine)
    normed_a, scaled_a = normed_of(tokens, small), scaled_of(cotangent, small)
    far_xa = along(picked(send_a, normed_a), middle)
    near_xa, near_da = picked(keep_a, normed_a), picked(keep_a, scaled_a)
    send_da = picked(send_a, scaled_a)
    half_up, tokens_in, far_xa, send_da, near_xa, near_da, small_in = tie(
        half(up_weight), tokens_in, far_xa, send_da, near_xa, near_da, small_in
    )

    up_in = along(half_up, inward)
    far_da = along(send_da, middle)
    keep_b, send_b = places(small_in, mine), places(small_in, 1 - mine)
    normed_b = normed_of(tokens_in, small_in)
    send_xb, near_xb = picked(send_b, normed_b), picked(keep_b, normed_b)
    half_down, up_in, far_da, send_xb, near_xb = tie(
        half(down_weight), up_in, far_da, send_xb, near_xb
    )

    down_in = along(half_down, inward)
    far_xb = along(send_xb, middle)
    up_other = swap(up_in, "parts")
    cot_sent, down_in, far_xb, up_other = tie(cotangent, down_in, far_xb, up_other)

    cotangent_in = along(cot_sent, inward)
    down_other = swap(down_in, "parts")

    def joined(here, there):
        first, second = jnp.where(part == 0, here, there), jnp.where(part == 0, there, here)
        return jnp.concatenate([first, second], axis=0)

    up_out = lax.all_gather(joined(up_in, up_other), "tensor", axis=1, tiled=True)
    down_out = lax.all_gather(joined(down_in, down_other), "tensor", axis=0, tiled=True)
    rows_x = jnp.concatenate([far_xa, near_xa, near_xb, far_xb])

    def over_dp(value):
        return value.astype(jnp.float32) + swap(value, "dp").astype(jnp.float32)

    pre_own = rounded(contract(rows_x, up_own, 1, 0))
    pre_out = rounded(contract(rows_x, up_out, 1, 0))
    pre = jnp.concatenate([over_dp(pre_own), over_dp(pre_out)], axis=1)
    cotangent_in, pre_out, down_out = tie(cotangent_in, pre_out, down_out)

    scaled_b = scaled_of(cotangent_in, small_in)
    far_db = along(picked(send_b, scaled_b), middle)
    early = jnp.concatenate([far_da, near_da, picked(keep_b, scaled_b)])

    def back_of(rows):
        parts_of = [contract(rows, down_own, 1, 1), contract(rows, down_out, 1, 1)]
        return over_dp(rounded(jnp.concatenate(parts_of, axis=1)))

    back = jnp.concatenate([back_of(early), back_of(far_db)])
    rows_d = jnp.concatenate([early, far_db])
    act = rounded(jax.nn.silu(pre))
    dpre = rounded(back * slope(pre))
    unit = act.shape[1] // 2

    def row_grad(rows):
        own = contract(rows[:, :unit], up_own, 1, 1)
        return rounded(own + contract(rows[:, unit:], up_out, 1, 1))

    back_b = along(row_grad(dpre[3 * capacity :]), middle)
    back_a = along(row_grad(dpre[:capacity]), middle)
    near_grad = row_grad(dpre[capacity : 3 * capacity])

    def shared(terms, axis):
        size = terms.shape[axis] // 2
        own = lax.dynamic_slice_in_dim(terms, side * size, size, axis)
        other = lax.dynamic_slice_in_dim(terms, (1 - side) * size, size, axis)
        return rounded(own + swap(rounded(other), "tensor").astype(jnp.float32))

    down_far = along(shared(contract(act[:, unit:], rows_d, 0, 0), 0), outward)
    up_far = along(shared(contract(rows_x, dpre[:, unit:], 0, 0), 1), outward)
    down_near = shared(contract(act[:, :unit], rows_d, 0, 0), 0)
    up_near = shared(contract(rows_x, dpre[:, :unit], 0, 0), 1)

    def restored(keep, near, send, far):
        return rounded(contract(keep, near, 1, 0) + contract(send, far, 1, 0))

    back_b, back_a, down_far = tie(back_b, back_a, down_far)
    grad_b = restored(keep_b, near_grad[capacity:], send_b, back_b)
    grad_in = along(grad_b, outward)
    grad_a = restored(keep_a, near_grad[:capacity], send_a, back_a)

    def gain_of(grad, block, facts):
        block = block.astype(jnp.float32) * facts[0][:, None]
        return jnp.sum(grad.astype(jnp.float32) * block, axis=0)

    def inner_of(grad, block):
        gained = block.astype(jnp.float32) * norm_gain[None, :]
        return jnp.sum(gained * grad.astype(jnp.float32), axis=1)

    gain_terms = gain_of(grad_a, tokens, small) + gain_of(grad_b, tokens_in, small_in)
    gain_terms = gain_terms + swap(gain_terms, "tensor")
    gain_terms = gain_terms + along(gain_terms, middle)
    gain_grad = jnp.where(is_inner, gain_terms, along(gain_terms, outward))
    inner_ab = jnp.stack([inner_of(grad_a, tokens), inner_of(grad_b, tokens_in)])
    inner_ab = over_dp(inner_ab)
    inner = jnp.where(is_inner, inner_ab[0], along(inner_ab[1], outward))
    normed_grad = jnp.where(is_inner, grad_a, grad_in).astype(jnp.float32)
    scale = scale[:, None]
    cubed = scale * scale * scale
    token_grad = (
        cotangent.astype(jnp.float32)
        + scale * norm_gain[None, :] * normed_grad
        - token_f * cubed * inner[:, None] / width
    )
    up_grad = jnp.where(is_inner, up_near, up_far)
    down_grad = jnp.where(is_inner, down_near, down_far)
    return (rounded(token_grad), up_grad, down_grad, gain_grad, inner)


def solution(mesh):
    sizes = tuple(mesh.shape[name] for name in ("parts", "expert", "dp", "tensor"))
    body = local_line if sizes == (2, 4, 2, 2) else local
    in_specs = (
        P(("parts", "expert", "tensor"), "dp"),
        P(("parts", "expert", "tensor"), "dp"),
        P("dp"),
        P(("parts", "expert", "tensor"), None),
        P(("parts", "expert", "tensor")),
        P("dp", ("expert", "tensor")),
        P(("expert", "tensor"), "dp"),
    )
    out_specs = (
        P(("parts", "expert", "tensor"), "dp"),
        P(("parts", "dp"), ("expert", "tensor")),
        P(("parts", "expert", "tensor"), "dp"),
        P(("parts", "dp")),
        P(("parts", "expert", "tensor")),
    )
    return jax.shard_map(body, mesh=mesh, in_specs=in_specs, out_specs=out_specs, check_vma=False)
```

```python
import jax
import jax.numpy as jnp
from jax import lax
from jax.sharding import PartitionSpec as P


def slope(pre):
    sig = jax.nn.sigmoid(pre)
    return sig * (1.0 + pre * (1.0 - sig))


def contract(left, right, left_dim, right_dim):
    return lax.dot_general(
        left, right, (((left_dim,), (right_dim,)), ((), ())), preferred_element_type=jnp.float32
    )


def local(tokens, cotangent, norm_gain, expert_ids, combine_weight, up_weight, down_weight):
    n_expert = lax.axis_size("expert")
    groups = n_expert // 2
    count, piece = tokens.shape
    width = piece * lax.axis_size("dp")
    capacity = count * 5 // (4 * groups)
    token_f = tokens.astype(jnp.float32)
    squares = lax.psum(jnp.sum(token_f * token_f, axis=1, keepdims=True), "dp")
    scale = lax.rsqrt(squares / width + 1e-06)
    normed = (token_f * scale * norm_gain[None, :]).astype(jnp.bfloat16)
    scaled = (combine_weight[:, None] * cotangent.astype(jnp.float32)).astype(jnp.bfloat16)
    target = expert_ids[:, 0]
    hits = (target[:, None] == jnp.arange(groups, dtype=jnp.int32)[None, :]).astype(jnp.int32)
    slot = jnp.sum((jnp.cumsum(hits, axis=0) - 1) * hits, axis=1)
    flat_slot = target * capacity + slot
    places = (flat_slot[:, None] == jnp.arange(groups * capacity, dtype=jnp.int32)[None, :]).astype(
        jnp.bfloat16
    )
    packed_x = contract(places, normed, 0, 0).astype(jnp.bfloat16)
    packed_d = contract(places, scaled, 0, 0).astype(jnp.bfloat16)

    def outward(packed):
        return jnp.repeat(packed.reshape(groups, capacity, piece), 2, axis=0)

    sent_x, sent_d = (
        lax.all_to_all(outward(packed_x), "expert", split_axis=0, concat_axis=0, tiled=True),
        lax.all_to_all(outward(packed_d), "expert", split_axis=0, concat_axis=0, tiled=True),
    )
    rows_x = sent_x.reshape(-1, piece)
    rows_d = sent_d.reshape(-1, piece)
    full_up, full_down = (
        lax.all_gather(up_weight, "tensor", axis=1, tiled=True),
        lax.all_gather(down_weight, "tensor", axis=0, tiled=True),
    )
    up_part = jnp.dot(rows_x, full_up, preferred_element_type=jnp.float32)
    back_part = contract(rows_d, full_down, 1, 1)
    pre, back = (
        lax.psum(up_part.astype(jnp.bfloat16), "dp").astype(jnp.float32),
        lax.psum(back_part.astype(jnp.bfloat16), "dp").astype(jnp.float32),
    )
    act = jax.nn.silu(pre).astype(jnp.bfloat16)
    dpre = (back * slope(pre)).astype(jnp.bfloat16)
    down_terms = contract(act, rows_d, 0, 0)
    up_terms = contract(rows_x, dpre, 0, 0)
    down_sum, up_sum = (
        lax.psum_scatter(
            down_terms.astype(jnp.bfloat16), "tensor", scatter_dimension=0, tiled=True
        ).astype(jnp.float32),
        lax.psum_scatter(
            up_terms.astype(jnp.bfloat16), "tensor", scatter_dimension=1, tiled=True
        ).astype(jnp.float32),
    )
    down_grad = down_sum.astype(jnp.bfloat16)
    up_grad = up_sum.astype(jnp.bfloat16)
    row_grad = contract(dpre, full_up, 1, 1).astype(jnp.bfloat16)
    returned = lax.all_to_all(
        row_grad.reshape(n_expert, capacity, piece),
        "expert",
        split_axis=0,
        concat_axis=0,
        tiled=True,
    )
    returned = returned.reshape(groups, 2, capacity, piece).astype(jnp.float32)
    merged = (returned[:, 0] + returned[:, 1]).reshape(groups * capacity, piece)
    normed_grad = jnp.take(merged, flat_slot, axis=0)
    gain_terms = jnp.sum(normed_grad * token_f * scale, axis=0)
    gain_grad = lax.psum(gain_terms, ("expert", "tensor"))
    inner_part = jnp.sum(token_f * norm_gain[None, :] * normed_grad, axis=1, keepdims=True)
    inner = lax.psum(inner_part, "dp")
    cubed = scale * scale * scale
    token_grad = (
        cotangent.astype(jnp.float32)
        + scale * norm_gain[None, :] * normed_grad
        - token_f * cubed * inner / width
    )
    return (token_grad.astype(jnp.bfloat16), up_grad, down_grad, gain_grad, inner[:, 0])


def swap(value, axis):
    return lax.ppermute(value, axis, ((0, 1), (1, 0)))


def tie(*values):
    return lax.optimization_barrier(values)


def rounded(value):
    return value.astype(jnp.bfloat16)


def local_line(
    tokens, cotangent, norm_gain, expert_ids, combine_weight, up_weight, down_weight
):
    count, piece = tokens.shape
    width = piece * 2
    capacity = count * 5 // 8
    inward, middle, outward = ((0, 1), (3, 2)), ((1, 2), (2, 1)), ((1, 0), (2, 3))
    place = lax.axis_index("expert")
    mine = place // 2
    is_inner = (place == 1) | (place == 2)
    part = lax.axis_index("parts")
    side = lax.axis_index("tensor")

    def along(value, pairs):
        return lax.ppermute(value, "expert", pairs)

    def half(weight):
        size = weight.shape[0] // 2
        return lax.dynamic_slice_in_dim(weight, part * size, size, 0)

    tokens_in = along(tokens, inward)
    up_own = lax.all_gather(up_weight, "tensor", axis=1, tiled=True)
    down_own = lax.all_gather(down_weight, "tensor", axis=0, tiled=True)
    token_f = tokens.astype(jnp.float32)
    squares = lax.psum(jnp.sum(token_f * token_f, axis=1), "dp")
    scale = lax.rsqrt(squares / width + 1e-06)
    small = jnp.stack([scale, combine_weight, expert_ids[:, 0].astype(jnp.float32)])
    small_in = along(small, inward)

    def places(facts, expert):
        hit = facts[2].astype(jnp.int32) == expert
        slot = jnp.where(hit, jnp.cumsum(hit.astype(jnp.int32)) - 1, -1)
        return rounded(slot[:, None] == jnp.arange(capacity, dtype=jnp.int32)[None, :])

    def normed_of(block, facts):
        return rounded(block.astype(jnp.float32) * facts[0][:, None] * norm_gain[None, :])

    def scaled_of(block, facts):
        return rounded(facts[1][:, None] * block.astype(jnp.float32))

    def picked(where, rows):
        return rounded(contract(where, rows, 0, 0))

    keep_a, send_a = places(small, mine), places(small, 1 - mine)
    normed_a, scaled_a = normed_of(tokens, small), scaled_of(cotangent, small)
    far_xa = along(picked(send_a, normed_a), middle)
    near_xa, near_da = picked(keep_a, normed_a), picked(keep_a, scaled_a)
    send_da = picked(send_a, scaled_a)
    half_up, tokens_in, far_xa, send_da, near_xa, near_da, small_in = tie(
        half(up_weight), tokens_in, far_xa, send_da, near_xa, near_da, small_in
    )

    up_in = along(half_up, inward)
    far_da = along(send_da, middle)
    keep_b, send_b = places(small_in, mine), places(small_in, 1 - mine)
    normed_b = normed_of(tokens_in, small_in)
    send_xb, near_xb = picked(send_b, normed_b), picked(keep_b, normed_b)
    half_down, up_in, far_da, send_xb, near_xb = tie(
        half(down_weight), up_in, far_da, send_xb, near_xb
    )

    down_in = along(half_down, inward)
    far_xb = along(send_xb, middle)
    up_other = swap(up_in, "parts")
    cot_sent, down_in, far_xb, up_other = tie(cotangent, down_in, far_xb, up_other)

    cotangent_in = along(cot_sent, inward)
    down_other = swap(down_in, "parts")

    def joined(here, there):
        first, second = jnp.where(part == 0, here, there), jnp.where(part == 0, there, here)
        return jnp.concatenate([first, second], axis=0)

    up_out = lax.all_gather(joined(up_in, up_other), "tensor", axis=1, tiled=True)
    cotangent_in, down_other, up_out = tie(cotangent_in, down_other, up_out)
    down_out = lax.all_gather(joined(down_in, down_other), "tensor", axis=0, tiled=True)
    rows_x = jnp.concatenate([far_xa, near_xa, near_xb, far_xb])

    def over_dp(value):
        return value.astype(jnp.float32) + swap(value, "dp").astype(jnp.float32)

    pre_own = rounded(contract(rows_x, up_own, 1, 0))
    pre_out = rounded(contract(rows_x, up_out, 1, 0))
    pre = jnp.concatenate([over_dp(pre_own), over_dp(pre_out)], axis=1)

    scaled_b = scaled_of(cotangent_in, small_in)
    far_db = along(picked(send_b, scaled_b), middle)
    early = jnp.concatenate([far_da, near_da, picked(keep_b, scaled_b)])

    def back_of(rows):
        parts_of = [contract(rows, down_own, 1, 1), contract(rows, down_out, 1, 1)]
        return over_dp(rounded(jnp.concatenate(parts_of, axis=1)))

    back = jnp.concatenate([back_of(early), back_of(far_db)])
    rows_d = jnp.concatenate([early, far_db])
    act = rounded(jax.nn.silu(pre))
    dpre = rounded(back * slope(pre))
    unit = act.shape[1] // 2

    def row_grad(rows):
        own = contract(rows[:, :unit], up_own, 1, 1)
        return rounded(own + contract(rows[:, unit:], up_out, 1, 1))

    back_b = along(row_grad(dpre[3 * capacity :]), middle)
    back_a = along(row_grad(dpre[:capacity]), middle)
    near_grad = row_grad(dpre[capacity : 3 * capacity])

    def shared(terms, axis):
        size = terms.shape[axis] // 2
        own = lax.dynamic_slice_in_dim(terms, side * size, size, axis)
        other = lax.dynamic_slice_in_dim(terms, (1 - side) * size, size, axis)
        return rounded(own + swap(rounded(other), "tensor").astype(jnp.float32))

    down_far = along(shared(contract(act[:, unit:], rows_d, 0, 0), 0), outward)
    up_far = along(shared(contract(rows_x, dpre[:, unit:], 0, 0), 1), outward)
    down_near = shared(contract(act[:, :unit], rows_d, 0, 0), 0)
    up_near = shared(contract(rows_x, dpre[:, :unit], 0, 0), 1)

    def restored(keep, near, send, far):
        return rounded(contract(keep, near, 1, 0) + contract(send, far, 1, 0))

    back_a, down_far = tie(back_a, down_far)
    grad_b = restored(keep_b, near_grad[capacity:], send_b, back_b)
    grad_in = along(grad_b, outward)
    grad_a = restored(keep_a, near_grad[:capacity], send_a, back_a)

    def gain_of(grad, block, facts):
        block = block.astype(jnp.float32) * facts[0][:, None]
        return jnp.sum(grad.astype(jnp.float32) * block, axis=0)

    def inner_of(grad, block):
        gained = block.astype(jnp.float32) * norm_gain[None, :]
        return jnp.sum(gained * grad.astype(jnp.float32), axis=1)

    gain_terms = gain_of(grad_a, tokens, small) + gain_of(grad_b, tokens_in, small_in)
    gain_terms = gain_terms + swap(gain_terms, "tensor")
    gain_terms = gain_terms + along(gain_terms, middle)
    gain_grad = jnp.where(is_inner, gain_terms, along(gain_terms, outward))
    inner_ab = jnp.stack([inner_of(grad_a, tokens), inner_of(grad_b, tokens_in)])
    inner_ab = over_dp(inner_ab)
    inner = jnp.where(is_inner, inner_ab[0], along(inner_ab[1], outward))
    normed_grad = jnp.where(is_inner, grad_a, grad_in).astype(jnp.float32)
    scale = scale[:, None]
    cubed = scale * scale * scale
    token_grad = (
        cotangent.astype(jnp.float32)
        + scale * norm_gain[None, :] * normed_grad
        - token_f * cubed * inner[:, None] / width
    )
    up_grad = jnp.where(is_inner, up_near, up_far)
    down_grad = jnp.where(is_inner, down_near, down_far)
    return (rounded(token_grad), up_grad, down_grad, gain_grad, inner)


def solution(mesh):
    sizes = tuple(mesh.shape[name] for name in ("parts", "expert", "dp", "tensor"))
    body = local_line if sizes == (2, 4, 2, 2) else local
    in_specs = (
        P(("parts", "expert", "tensor"), "dp"),
        P(("parts", "expert", "tensor"), "dp"),
        P("dp"),
        P(("parts", "expert", "tensor"), None),
        P(("parts", "expert", "tensor")),
        P("dp", ("expert", "tensor")),
        P(("expert", "tensor"), "dp"),
    )
    out_specs = (
        P(("parts", "expert", "tensor"), "dp"),
        P(("parts", "dp"), ("expert", "tensor")),
        P(("parts", "expert", "tensor"), "dp"),
        P(("parts", "dp")),
        P(("parts", "expert", "tensor")),
    )
    return jax.shard_map(body, mesh=mesh, in_specs=in_specs, out_specs=out_specs, check_vma=False)
```

```python
import jax
import jax.numpy as jnp
from jax import lax
from jax.sharding import PartitionSpec as P


def slope(pre):
    sig = jax.nn.sigmoid(pre)
    return sig * (1.0 + pre * (1.0 - sig))


def contract(left, right, left_dim, right_dim):
    return lax.dot_general(
        left, right, (((left_dim,), (right_dim,)), ((), ())), preferred_element_type=jnp.float32
    )


def local(tokens, cotangent, norm_gain, expert_ids, combine_weight, up_weight, down_weight):
    n_expert = lax.axis_size("expert")
    groups = n_expert // 2
    count, piece = tokens.shape
    width = piece * lax.axis_size("dp")
    capacity = count * 5 // (4 * groups)
    token_f = tokens.astype(jnp.float32)
    squares = lax.psum(jnp.sum(token_f * token_f, axis=1, keepdims=True), "dp")
    scale = lax.rsqrt(squares / width + 1e-06)
    normed = (token_f * scale * norm_gain[None, :]).astype(jnp.bfloat16)
    scaled = (combine_weight[:, None] * cotangent.astype(jnp.float32)).astype(jnp.bfloat16)
    target = expert_ids[:, 0]
    hits = (target[:, None] == jnp.arange(groups, dtype=jnp.int32)[None, :]).astype(jnp.int32)
    slot = jnp.sum((jnp.cumsum(hits, axis=0) - 1) * hits, axis=1)
    flat_slot = target * capacity + slot
    places = (flat_slot[:, None] == jnp.arange(groups * capacity, dtype=jnp.int32)[None, :]).astype(
        jnp.bfloat16
    )
    packed_x = contract(places, normed, 0, 0).astype(jnp.bfloat16)
    packed_d = contract(places, scaled, 0, 0).astype(jnp.bfloat16)

    def outward(packed):
        return jnp.repeat(packed.reshape(groups, capacity, piece), 2, axis=0)

    sent_x, sent_d = (
        lax.all_to_all(outward(packed_x), "expert", split_axis=0, concat_axis=0, tiled=True),
        lax.all_to_all(outward(packed_d), "expert", split_axis=0, concat_axis=0, tiled=True),
    )
    rows_x = sent_x.reshape(-1, piece)
    rows_d = sent_d.reshape(-1, piece)
    full_up, full_down = (
        lax.all_gather(up_weight, "tensor", axis=1, tiled=True),
        lax.all_gather(down_weight, "tensor", axis=0, tiled=True),
    )
    up_part = jnp.dot(rows_x, full_up, preferred_element_type=jnp.float32)
    back_part = contract(rows_d, full_down, 1, 1)
    pre, back = (
        lax.psum(up_part.astype(jnp.bfloat16), "dp").astype(jnp.float32),
        lax.psum(back_part.astype(jnp.bfloat16), "dp").astype(jnp.float32),
    )
    act = jax.nn.silu(pre).astype(jnp.bfloat16)
    dpre = (back * slope(pre)).astype(jnp.bfloat16)
    down_terms = contract(act, rows_d, 0, 0)
    up_terms = contract(rows_x, dpre, 0, 0)
    down_sum, up_sum = (
        lax.psum_scatter(
            down_terms.astype(jnp.bfloat16), "tensor", scatter_dimension=0, tiled=True
        ).astype(jnp.float32),
        lax.psum_scatter(
            up_terms.astype(jnp.bfloat16), "tensor", scatter_dimension=1, tiled=True
        ).astype(jnp.float32),
    )
    down_grad = down_sum.astype(jnp.bfloat16)
    up_grad = up_sum.astype(jnp.bfloat16)
    row_grad = contract(dpre, full_up, 1, 1).astype(jnp.bfloat16)
    returned = lax.all_to_all(
        row_grad.reshape(n_expert, capacity, piece),
        "expert",
        split_axis=0,
        concat_axis=0,
        tiled=True,
    )
    returned = returned.reshape(groups, 2, capacity, piece).astype(jnp.float32)
    merged = (returned[:, 0] + returned[:, 1]).reshape(groups * capacity, piece)
    normed_grad = jnp.take(merged, flat_slot, axis=0)
    gain_terms = jnp.sum(normed_grad * token_f * scale, axis=0)
    gain_grad = lax.psum(gain_terms, ("expert", "tensor"))
    inner_part = jnp.sum(token_f * norm_gain[None, :] * normed_grad, axis=1, keepdims=True)
    inner = lax.psum(inner_part, "dp")
    cubed = scale * scale * scale
    token_grad = (
        cotangent.astype(jnp.float32)
        + scale * norm_gain[None, :] * normed_grad
        - token_f * cubed * inner / width
    )
    return (token_grad.astype(jnp.bfloat16), up_grad, down_grad, gain_grad, inner[:, 0])


def swap(value, axis):
    return lax.ppermute(value, axis, ((0, 1), (1, 0)))


def tie(*values):
    return lax.optimization_barrier(values)


def rounded(value):
    return value.astype(jnp.bfloat16)


def local_line(
    tokens, cotangent, norm_gain, expert_ids, combine_weight, up_weight, down_weight
):
    count, piece = tokens.shape
    width = piece * 2
    capacity = count * 5 // 8
    inward, middle, outward = ((0, 1), (3, 2)), ((1, 2), (2, 1)), ((1, 0), (2, 3))
    place = lax.axis_index("expert")
    mine = place // 2
    is_inner = (place == 1) | (place == 2)
    part = lax.axis_index("parts")
    side = lax.axis_index("tensor")

    def along(value, pairs):
        return lax.ppermute(value, "expert", pairs)

    def half(weight):
        size = weight.shape[0] // 2
        return lax.dynamic_slice_in_dim(weight, part * size, size, 0)

    tokens_in = along(tokens, inward)
    up_own = lax.all_gather(up_weight, "tensor", axis=1, tiled=True)
    down_own = lax.all_gather(down_weight, "tensor", axis=0, tiled=True)
    token_f = tokens.astype(jnp.float32)
    squares = lax.psum(jnp.sum(token_f * token_f, axis=1), "dp")
    scale = lax.rsqrt(squares / width + 1e-06)
    small = jnp.stack([scale, combine_weight, expert_ids[:, 0].astype(jnp.float32)])
    small_in = along(small, inward)

    def places(facts, expert):
        hit = facts[2].astype(jnp.int32) == expert
        slot = jnp.where(hit, jnp.cumsum(hit.astype(jnp.int32)) - 1, -1)
        return rounded(slot[:, None] == jnp.arange(capacity, dtype=jnp.int32)[None, :])

    def normed_of(block, facts):
        return rounded(block.astype(jnp.float32) * facts[0][:, None] * norm_gain[None, :])

    def scaled_of(block, facts):
        return rounded(facts[1][:, None] * block.astype(jnp.float32))

    def picked(where, rows):
        return rounded(contract(where, rows, 0, 0))

    keep_a, send_a = places(small, mine), places(small, 1 - mine)
    normed_a, scaled_a = normed_of(tokens, small), scaled_of(cotangent, small)
    far_xa = along(picked(send_a, normed_a), middle)
    near_xa, near_da = picked(keep_a, normed_a), picked(keep_a, scaled_a)
    send_da = picked(send_a, scaled_a)
    half_up, tokens_in, far_xa, send_da, near_xa, near_da, small_in = tie(
        half(up_weight), tokens_in, far_xa, send_da, near_xa, near_da, small_in
    )

    up_in = along(half_up, inward)
    far_da = along(send_da, middle)
    keep_b, send_b = places(small_in, mine), places(small_in, 1 - mine)
    normed_b = normed_of(tokens_in, small_in)
    send_xb, near_xb = picked(send_b, normed_b), picked(keep_b, normed_b)
    half_down, up_in, far_da, send_xb, near_xb = tie(
        half(down_weight), up_in, far_da, send_xb, near_xb
    )

    down_in = along(half_down, inward)
    far_xb = along(send_xb, middle)
    up_other = swap(up_in, "parts")
    cot_sent, down_in, far_xb, up_other = tie(cotangent, down_in, far_xb, up_other)

    cotangent_in = along(cot_sent, inward)
    down_other = swap(down_in, "parts")

    def joined(here, there):
        first, second = jnp.where(part == 0, here, there), jnp.where(part == 0, there, here)
        return jnp.concatenate([first, second], axis=0)

    up_out = lax.all_gather(joined(up_in, up_other), "tensor", axis=1, tiled=True)
    cotangent_in, down_other, up_out = tie(cotangent_in, down_other, up_out)
    down_out = lax.all_gather(joined(down_in, down_other), "tensor", axis=0, tiled=True)
    rows_x = jnp.concatenate([far_xa, near_xa, near_xb, far_xb])

    def over_dp(value):
        return value.astype(jnp.float32) + swap(value, "dp").astype(jnp.float32)

    pre_own = rounded(contract(rows_x, up_own, 1, 0))
    pre_out = rounded(contract(rows_x, up_out, 1, 0))
    pre = jnp.concatenate([over_dp(pre_own), over_dp(pre_out)], axis=1)

    scaled_b = scaled_of(cotangent_in, small_in)
    far_db = along(picked(send_b, scaled_b), middle)
    early = jnp.concatenate([far_da, near_da, picked(keep_b, scaled_b)])

    def back_of(rows):
        parts_of = [contract(rows, down_own, 1, 1), contract(rows, down_out, 1, 1)]
        return over_dp(rounded(jnp.concatenate(parts_of, axis=1)))

    back = jnp.concatenate([back_of(early), back_of(far_db)])
    rows_d = jnp.concatenate([early, far_db])
    act = rounded(jax.nn.silu(pre))
    dpre = rounded(back * slope(pre))
    unit = act.shape[1] // 2

    def row_grad(rows):
        own = contract(rows[:, :unit], up_own, 1, 1)
        return rounded(own + contract(rows[:, unit:], up_out, 1, 1))

    back_b = along(row_grad(dpre[3 * capacity :]), middle)
    back_a = along(row_grad(dpre[:capacity]), middle)
    near_grad = row_grad(dpre[capacity : 3 * capacity])

    def shared(terms, axis):
        size = terms.shape[axis] // 2
        own = lax.dynamic_slice_in_dim(terms, side * size, size, axis)
        other = lax.dynamic_slice_in_dim(terms, (1 - side) * size, size, axis)
        return rounded(own + swap(rounded(other), "tensor").astype(jnp.float32))

    down_far = along(shared(contract(act[:, unit:], rows_d, 0, 0), 0), outward)
    up_far = along(shared(contract(rows_x, dpre[:, unit:], 0, 0), 1), outward)
    down_near = shared(contract(act[:, :unit], rows_d, 0, 0), 0)
    up_near = shared(contract(rows_x, dpre[:, :unit], 0, 0), 1)

    def restored(keep, near, send, far):
        return rounded(contract(keep, near, 1, 0) + contract(send, far, 1, 0))

    back_b, back_a, down_far = tie(back_b, back_a, down_far)
    grad_b = restored(keep_b, near_grad[capacity:], send_b, back_b)
    grad_in = along(grad_b, outward)
    grad_a = restored(keep_a, near_grad[:capacity], send_a, back_a)

    def gain_of(grad, block, facts):
        block = block.astype(jnp.float32) * facts[0][:, None]
        return jnp.sum(grad.astype(jnp.float32) * block, axis=0)

    def inner_of(grad, block):
        gained = block.astype(jnp.float32) * norm_gain[None, :]
        return jnp.sum(gained * grad.astype(jnp.float32), axis=1)

    gain_terms = gain_of(grad_a, tokens, small) + gain_of(grad_b, tokens_in, small_in)
    gain_terms = gain_terms + swap(gain_terms, "tensor")
    gain_terms = gain_terms + along(gain_terms, middle)
    gain_grad = jnp.where(is_inner, gain_terms, along(gain_terms, outward))
    inner_ab = jnp.stack([inner_of(grad_a, tokens), inner_of(grad_b, tokens_in)])
    inner_ab = over_dp(inner_ab)
    inner = jnp.where(is_inner, inner_ab[0], along(inner_ab[1], outward))
    normed_grad = jnp.where(is_inner, grad_a, grad_in).astype(jnp.float32)
    scale = scale[:, None]
    cubed = scale * scale * scale
    token_grad = (
        cotangent.astype(jnp.float32)
        + scale * norm_gain[None, :] * normed_grad
        - token_f * cubed * inner[:, None] / width
    )
    up_grad = jnp.where(is_inner, up_near, up_far)
    down_grad = jnp.where(is_inner, down_near, down_far)
    return (rounded(token_grad), up_grad, down_grad, gain_grad, inner)


def solution(mesh):
    sizes = tuple(mesh.shape[name] for name in ("parts", "expert", "dp", "tensor"))
    body = local_line if sizes == (2, 4, 2, 2) else local
    in_specs = (
        P(("parts", "expert", "tensor"), "dp"),
        P(("parts", "expert", "tensor"), "dp"),
        P("dp"),
        P(("parts", "expert", "tensor"), None),
        P(("parts", "expert", "tensor")),
        P("dp", ("expert", "tensor")),
        P(("expert", "tensor"), "dp"),
    )
    out_specs = (
        P(("parts", "expert", "tensor"), "dp"),
        P(("parts", "dp"), ("expert", "tensor")),
        P(("parts", "expert", "tensor"), "dp"),
        P(("parts", "dp")),
        P(("parts", "expert", "tensor")),
    )
    return jax.shard_map(body, mesh=mesh, in_specs=in_specs, out_specs=out_specs, check_vma=False)
```
